256 devices in a mesh: replica: 8 (over x_hi, y), fsdp: 32 (over x_lo, z, core).
Axes of the slice: x: 4 (x_hi: 2, x_lo: 2; x = x_hi * 2 + x_lo), y: 4, z: 8, core: 2. Of those that a mesh axis runs over, the one named last changes fastest.
Arguments:
- activations: bfloat16 [98304, 4096], P(('replica', 'fsdp')), may hold values from -24 to 24
- cotangent: bfloat16 [98304, 1024], P(('replica', 'fsdp')), may hold values from -6 to 6
- inner_weight: bfloat16 [8, 4096, 1024], P('replica', 'fsdp'), may hold values from -0.09375 to 0.09375
- outer_params: float32 [4096, 1024], P('fsdp'), may hold values from -6 to 6
- replica_params: float32 [8, 4096, 1024], P('replica', 'fsdp'), may hold values from -6 to 6
- momentum: float32 [4096, 1024], P('fsdp'), may hold values from -3 to 3
Outputs:
- values: bfloat16 [98304, 1024], P(('replica', 'fsdp'))
- input_grad: bfloat16 [98304, 4096], P(('replica', 'fsdp'))
- weight_grad: float32 [8, 4096, 1024], P('replica', 'fsdp')
- new_params: float32 [4096, 1024], P('fsdp')
- new_momentum: float32 [4096, 1024], P('fsdp')
The draws below stay inside these ranges and needn't reach their ends.
All inputs are finite; a program needn't handle non-finite values.
Results may differ from the reference program's by a relative error of at most 0.001.
Values may be sent and summed in bfloat16 or wider, within the bound.
A program may use at most 128 MiB of HBM per device.

```python
import math
import jax
import jax.numpy as jnp
from jax import lax

D = 4096
KV = 1024
TOK_DEV = 384
TOKENS = 98304
N_REPLICA = 8
N_FSDP = 32


def strengthened(drawn, key, source, target, blocks, factor):
    owner, partner = [(jnp.arange(drawn.shape[axis_at]) // (drawn.shape[axis_at] // blocks)).reshape([-1 if axis == axis_at else 1 for axis in range(drawn.ndim)]) for axis_at in (source, target)]
    chosen = jax.random.permutation(key, blocks)[partner]
    strong = (owner == chosen) | (owner == (partner + blocks // 2) % blocks)
    return jnp.where(strong, factor * drawn, drawn)


def shard_levels(own_key, extent, split, least, top_value):
    factor_of, own = 1.0, jax.random.fold_in(own_key, 6)
    for position, parts in split:
        draws = jnp.exp(jax.random.uniform(jax.random.fold_in(own, position), (parts,), jnp.float32, least / len(split), top_value / len(split)))
        factor_of = factor_of * jnp.repeat(draws, extent[position] // parts).reshape([-1 if axis == position else 1 for axis in range(len(extent))])
    return factor_of


def gaussian(stream_key, dims, deviation, most, cuts=(), dtype=jnp.bfloat16):
    result = jax.random.normal(stream_key, dims, jnp.float32) * deviation
    if len(cuts) > 0:
        result = shard_levels(stream_key, dims, cuts, -0.22, 0.18) * result
    return jnp.clip(result, min=-most, max=most).astype(dtype)


def gaussian_with(rng, extent, scale, bound, shards, heavy, held_as=jnp.bfloat16):
    entries = scale * jax.random.normal(rng, extent, jnp.float32)
    if shards:
        entries = entries * shard_levels(rng, extent, shards, -0.22, 0.18)
    return jnp.clip(strengthened(entries, jax.random.fold_in(rng, 3), *heavy), -bound, bound).astype(held_as)


def setup_inputs(seed: int = 0) -> dict:
    key_of = jax.random.split(jax.random.key(seed), 7)
    return {
        "activations": gaussian_with(key_of[0], (TOKENS, D), 1.0, 24.0, ((0, 256),), (0, 1, 256, 6.0)),
        "cotangent": gaussian(key_of[1], (TOKENS, KV), 1.0, 6.0, ((0, 256),)),
        "inner_weight": gaussian(key_of[2], (N_REPLICA, D, KV), D ** -0.5, 0.09375, ((0, 8), (1, 32))),
        "outer_params": gaussian(key_of[3], (D, KV), 1.0, 6.0, ((0, 32),), jnp.float32),
        "replica_params": gaussian(key_of[4], (N_REPLICA, D, KV), 1.0, 6.0, ((0, 8), (1, 32)), jnp.float32),
        "momentum": gaussian(key_of[5], (D, KV), 0.5, 3.0, ((0, 32),), jnp.float32),
    }


def replica_pass(operands):
    tokens_rep, cotan_rep, weight_rep = operands
    outputs = jnp.dot(tokens_rep, weight_rep, preferred_element_type=jnp.float32).astype(jnp.bfloat16)
    input_back = lax.dot_general(cotan_rep, weight_rep, (((1,), (1,)), ((), ())), preferred_element_type=jnp.float32).astype(jnp.bfloat16)
    token_blocks = tokens_rep.reshape(N_FSDP, TOK_DEV, D)
    cotan_blocks = cotan_rep.reshape(N_FSDP, TOK_DEV, KV)

    def accumulate(running, block_pair):
        block_tokens, block_cotan = block_pair
        partial_grad = lax.dot_general(block_tokens, block_cotan, (((0,), (0,)), ((), ())), preferred_element_type=jnp.float32)
        return (running + partial_grad, None)
    summed, unused = lax.scan(accumulate, jnp.zeros((D, KV), jnp.float32), (token_blocks, cotan_blocks))
    grad_scale = 1.0 / math.sqrt(TOK_DEV * N_FSDP)
    return (outputs, input_back, summed * grad_scale)

def reference(activations, cotangent, inner_weight, outer_params, replica_params, momentum):
    tokens_all = activations.reshape(N_REPLICA, TOK_DEV * N_FSDP, D)
    cotan_all = cotangent.reshape(N_REPLICA, TOK_DEV * N_FSDP, KV)
    outputs, input_back, weight_grad = lax.map(replica_pass, (tokens_all, cotan_all, inner_weight))
    values = outputs.reshape(TOKENS, KV)
    input_grad = input_back.reshape(TOKENS, D)
    outer_grad = lax.optimization_barrier(jnp.sum(outer_params[None] - replica_params, axis=0)) / N_REPLICA
    new_momentum = 0.9 * momentum + outer_grad
    new_params = outer_params - 0.7 * (outer_grad + 0.9 * new_momentum)
    return (values, input_grad, weight_grad, new_params, new_momentum)
```

```python
import functools
import math

import jax
import jax.numpy as jnp
from jax import lax
from jax.experimental import pallas as pl
from jax.experimental.pallas import tpu as pltpu
from jax.sharding import PartitionSpec as P

MESH = pl.DeviceIdType.MESH
F32 = jnp.float32
BF16 = jnp.bfloat16

NZ = 8
SH = 128
HF = 64
QT = 32
BLK = 16


def encode(v):
    a = v * v
    b = a * a
    return (b * a * (v * jnp.abs(v))).astype(BF16)


def decode(q):
    t = q.astype(F32)
    a = lax.rsqrt(lax.rsqrt(jnp.maximum(jnp.abs(t), 1e-37)))
    r = a * lax.rsqrt(a)
    return jnp.where(t < 0, -r, r)


def kernel(
    grad_scale,
    x_in, g_in, w_in, op_in, rp_in, mom_in,
    val_out, dx_out, dw_out, np_out, nm_out,
    xv, xs, gs, W, part, zq, zr, xq, xr, dxv, acc, valv, dwv,
    opv, rpv, momv, diff, ryv, xhv, tot, mine, mxr, mzr,
    load_sem, xs_sem, out_sem, dx_sem,
    agz_s, agz_r, agx_s, agx_r, sib_s, sib_r, tok_s, tok_r,
    rsz_s, rsz_r, rsx_s, rsx_r, mx_s, mx_r, rep_s, rep_r,
):
    r = lax.axis_index("replica")
    f = lax.axis_index("fsdp")
    xh, y = r // 4, r % 4
    x, z, c = f // 16, (f // 2) % NZ, f % 2
    ox, oc = 1 - x, 1 - c

    def zmod(v):
        return (v + 2 * NZ) % NZ

    def dev(xx, zz, cc):
        return (r, xx * 16 + zz * 2 + cc)

    def rep(hh, yy):
        return (hh * 4 + yy, f)

    def idx(xx, zz):
        return xx * NZ + zz

    x_nb, sib = dev(ox, z, c), dev(x, z, oc)
    z_nb = (dev(x, zmod(z + 1), c), dev(x, zmod(z - 1), c))
    xh_nb = rep(1 - xh, y)

    def remote(src, dst, ss, rs, to):
        return pltpu.make_async_remote_copy(
            src_ref=src, dst_ref=dst, send_sem=ss, recv_sem=rs, device_id=to, device_id_type=MESH
        )

    def cols(j, cc):
        return pl.ds(pl.multiple_of(j * 256 + cc * SH, SH), SH)

    loads = [
        pltpu.make_async_copy(w_in.at[0], W.at[idx(x, z), pl.ds(pl.multiple_of(c * SH, SH), SH)], load_sem.at[0]),
        pltpu.make_async_copy(op_in, opv, load_sem.at[1]),
        pltpu.make_async_copy(rp_in.at[0], rpv, load_sem.at[2]),
        pltpu.make_async_copy(g_in, gs.at[pl.ds(0, 384)], load_sem.at[3]),
        pltpu.make_async_copy(x_in, xv, load_sem.at[4]),
        pltpu.make_async_copy(mom_in, momv, load_sem.at[5]),
    ]
    for copy in loads[:4]:
        copy.start()

    barrier = pltpu.get_barrier_semaphore()
    peers = [x_nb, sib, xh_nb]
    peers += [dev(x, zmod(z + j), c) for j in range(1, NZ)]
    peers += [rep(xh, (y + j) % 4) for j in range(1, 4)]
    for peer in peers:
        pl.semaphore_signal(barrier, inc=1, device_id=peer, device_id_type=MESH)
    pl.semaphore_wait(barrier, len(peers))

    def rows(p, k=1, way=0):
        if p == 1:
            if k == 4:
                return HF + QT * way, QT
            return HF, HF
        return 0, HF

    def wpiece(xx, zz, start, size, cc=None):
        cc = c if cc is None else cc
        return W.at[idx(xx, zz), pl.ds(pl.multiple_of(cc * SH + start, QT), size)]

    def far(way, k):
        return zmod(z - k) if way == 0 else zmod(z + k)

    def ag_z(way, k, p, at):
        start, size = rows(p, k, way)
        ref = wpiece(ox if p == 2 else x, at, start, size)
        return remote(ref, ref, agz_s.at[way, k - 1, p], agz_r.at[way, k - 1, p], z_nb[way])

    def ag_z_send(way, k, p):
        ag_z(way, k, p, far(way, k - 1)).start()

    def ag_z_wait(way, k, p):
        ag_z(way, k, p, far(way, k)).wait_recv()

    def ag_x(n, xx, zz, start, size):
        ref = wpiece(xx, zz, start, size)
        return remote(ref, ref, agx_s.at[n], agx_r.at[n], x_nb)

    def b_of(way, k):
        if k == 4:
            return 8 + way, HF + QT * way, QT
        return 2 + way * 3 + k - 1, HF, HF

    def ag_b_send(way, k):
        n, start, size = b_of(way, k)
        ag_x(n, x, far(way, k), start, size).start()

    def ag_b_wait(way, k):
        n, start, size = b_of(way, k)
        ag_x(n, ox, far(way, k), start, size).wait_recv()

    def sib_copy(xrel, o, cc):
        ref = wpiece(x if xrel == 0 else ox, zmod(z + o), 0, SH, cc)
        n = xrel * NZ + o
        return remote(ref, ref, sib_s.at[n], sib_r.at[n], sib)

    loads[0].wait()
    own_a = wpiece(x, z, 0, HF)
    ag_x(0, x, z, 0, HF).start()
    for way in (0, 1):
        ag_z_send(way, 1, 0)
    ag_x(1, x, z, HF, HF).start()
    for way in (0, 1):
        ag_z_send(way, 1, 1)

    @pl.loop(0, 16)
    def _(j):
        at = pl.ds(pl.multiple_of(j * SH, SH), SH)
        remote(x_in.at[:, cols(j, oc)], xs.at[pl.ds(384, 384), at], tok_s.at[0], tok_r.at[0], sib).start()
        pltpu.make_async_copy(x_in.at[:, cols(j, c)], xs.at[pl.ds(0, 384), at], xs_sem.at[0]).start()

    tok_g = remote(g_in, gs.at[pl.ds(384, 384)], tok_s.at[1], tok_r.at[1], sib)
    tok_g.start()
    sib_copy(0, 0, c).start()
    loads[4].start()
    loads[5].start()

    loads[1].wait()
    loads[2].wait()

    @pl.loop(0, SH // BLK)
    def _(i):
        at = pl.ds(pl.multiple_of(i * BLK, BLK), BLK)
        diff[at, :] = opv[at, :] - rpv[at, :]

    def quarter(yy):
        return pl.ds(pl.multiple_of(yy * QT, QT), QT)

    def rep_scatter(j):
        to = (y + j) % 4
        return remote(diff.at[quarter(to)], ryv.at[j - 1], rep_s.at[j - 1], rep_r.at[j - 1], rep(xh, to))

    for j in range(1, 4):
        rep_scatter(j).start()

    ag_x(0, ox, z, 0, HF).wait_recv()
    for way in (0, 1):
        ag_z_send(way, 1, 2)

    loads[3].wait()
    tok_x = remote(xs.at[pl.ds(384, 384)], xs.at[pl.ds(384, 384)], tok_s.at[0], tok_r.at[0], sib)
    pltpu.make_async_copy(xs.at[pl.ds(0, 384)], xs.at[pl.ds(0, 384)], xs_sem.at[0]).wait()
    tok_g.wait_recv()
    tok_x.wait_recv()

    def partial(first, last):
        @pl.loop(first, last)
        def _(i):
            at = pl.ds(pl.multiple_of(i * 512, 512), 512)
            part[pl.ds(i * 4, 4)] = lax.dot_general(
                xs[:, at], gs[...], (((0,), (0,)), ((), ())), preferred_element_type=F32
            ).reshape(4, SH, 1024)

    def use(*offsets):
        for o in offsets:
            for xrel in (0, 1):
                sib_copy(xrel, o, oc).wait_recv()
        n = len(offsets)
        first, step = offsets[0], (offsets[1] - offsets[0] if n > 1 else 0)

        @pl.loop(0, 2 * n)
        def _(t):
            o = first + (t // 2) * step
            i = t % 2
            xx = x * (1 - i) + ox * i
            products_at(idx(xx, zmod(z + o)))

    def products_at(i):
        at = pl.ds(pl.multiple_of(i * 256, 256), 256)
        w = W[i]
        dxv[:, at] = lax.dot_general(
            gs[pl.ds(0, 384), :], w, (((1,), (1,)), ((), ())), preferred_element_type=F32
        ).astype(BF16)
        pltpu.make_async_copy(dxv.at[:, at], dx_out.at[:, at], dx_sem.at[0]).start()
        acc[...] += jnp.dot(xv[:, at], w, preferred_element_type=F32)

    def forward(k, p):
        for way in (0, 1):
            ag_z_wait(way, k, p)
            if k < 3 or p == 1 or (way, p) in ((0, 0), (1, 2)):
                ag_z_send(way, k + 1, p)
            if p == 1:
                ag_b_send(way, k)

    def off(way, k):
        return (NZ - k) % NZ if way == 0 else k

    def to_sib(k):
        for way in (0, 1):
            sib_copy(0, off(way, k), c).start()

    def to_sib_other(k):
        for way in (0, 1):
            ag_b_wait(way, k)
            sib_copy(1, off(way, k), c).start()

    partial(0, 2)
    forward(1, 0)
    partial(2, 3)
    forward(1, 1)
    to_sib(1)
    partial(3, 4)
    forward(1, 2)

    ag_x(1, ox, z, HF, HF).wait_recv()
    sib_copy(1, 0, c).start()

    mine[...] = jnp.zeros_like(mine)

    @pl.loop(0, 16 * SH // BLK)
    def _(i):
        v = jnp.abs(part[i // (SH // BLK), pl.ds(pl.multiple_of((i % (SH // BLK)) * BLK, BLK), BLK), :])
        v = jnp.maximum(v[0:8], v[8:16])
        m = mine[...]
        for j in range(8):
            m = jnp.maximum(m, v[:, j * 128 : (j + 1) * 128])
        mine[...] = m

    max_x = remote(mine, mxr, mx_s.at[0], mx_r.at[0], x_nb)
    max_x.start()

    for j in range(1, 4):
        rep_scatter(j).wait_recv()
    tot[quarter(y), :] = ((diff[quarter(y), :] + ryv[0]) + ryv[1]) + ryv[2]
    xhv[0] = tot[quarter(y), :]
    rep_x = remote(xhv.at[0], xhv.at[1], rep_s.at[3], rep_r.at[3], xh_nb)
    rep_x.start()

    max_x.wait()
    mine[...] = jnp.maximum(mine[...], mxr[...])

    def max_z(j):
        return remote(mine, mzr.at[j - 1], mx_s.at[j], mx_r.at[j], dev(x, zmod(z + j), c))

    for j in range(1, NZ):
        max_z(j).start()

    acc[...] = jnp.zeros_like(acc)
    loads[4].wait()
    forward(2, 0)
    to_sib_other(1)
    use(0)
    forward(2, 1)
    to_sib(2)
    use(1, 7)
    forward(2, 2)

    for j in range(1, NZ):
        max_z(j).wait()
    m = mine[...]
    for j in range(NZ - 1):
        m = jnp.maximum(m, mzr[j])
    top = jnp.maximum(jnp.full((8, 128), jnp.max(m), F32), 1e-30)
    scale = jnp.max(2048.0 / top)
    back = jnp.max(top * (grad_scale / 2048.0))

    def total(xx, zz, start, at, received):
        v = part[idx(xx, zz), pl.ds(pl.multiple_of(start + at, BLK), BLK), :] * scale
        for ref in received:
            v = v + decode(ref[pl.ds(pl.multiple_of(at, BLK), BLK), :])
        return v

    def summed(dst, xx, zz, start, size, received):
        @pl.loop(0, size // BLK)
        def _(i):
            at = pl.multiple_of(i * BLK, BLK)
            dst[pl.ds(at, BLK), :] = encode(total(xx, zz, start, at, received))

    def rs_x(n):
        return remote(xq.at[n], xr.at[n], rsx_s.at[n], rsx_r.at[n], x_nb)

    def rs_b_send(o):
        summed(xq.at[o], ox, zmod(z + o), HF, HF, [])
        rs_x(o).start()

    def rs_z(way, j, p):
        size = QT if (j == 0 and p == 1) else HF
        at = QT * way if (j == 0 and p == 1) else 0
        here, there = zq.at[way, j, p, pl.ds(at, size)], zr.at[way, j, p, pl.ds(at, size)]
        return remote(here, there, rsz_s.at[way, j, p], rsz_r.at[way, j, p], z_nb[way])

    def rs_send(way, j, p):
        o = 4 - j if way == 0 else (4 + j) % NZ
        zz, col = zmod(z + o), (ox if p == 2 else x)
        out, crossed = zq.at[way, j, p], xr.at[o]
        if p != 1:
            if j > 0 and not (j == 1 and (way, p) in ((0, 2), (1, 0))):
                rs_z(way, j - 1, p).wait_recv()
                received = [zr.at[way, j - 1, p]]
            else:
                received = []
            summed(out, col, zz, 0, HF, received)
        elif j >= 2:
            rs_z(way, j - 1, p).wait_recv()
            summed(out, col, zz, HF, HF, [crossed, zr.at[way, j - 1, p]])
        else:
            for half in (0, 1):
                at = pl.ds(QT * half, QT)
                if j == 0 and half == way:
                    summed(out.at[at], col, zz, HF + QT * half, QT, [crossed.at[at]])
                elif j == 1 and half == way:
                    rs_z(way, 0, p).wait_recv()
                    summed(out.at[at], col, zz, HF + QT * half, QT, [crossed.at[at], zr.at[way, 0, p, at]])
                elif j == 1:
                    summed(out.at[at], col, zz, HF + QT * half, QT, [crossed.at[at]])
        rs_z(way, j, p).start()

    for o in (4, 3, 5):
        rs_b_send(o)

    forward(3, 0)
    forward(3, 1)
    to_sib_other(2)
    to_sib(3)
    forward(3, 2)

    rs_send(0, 0, 0)
    rs_send(1, 0, 2)
    rs_x(4).wait_recv()
    rs_send(0, 0, 1)
    rs_send(1, 0, 1)
    for o in (2, 6):
        rs_b_send(o)

    rep_x.wait()
    tot[quarter(y), :] = xhv[0] + xhv[1]

    def rep_gather(j, at):
        ref = tot.at[quarter(at)]
        return remote(ref, ref, rep_s.at[3 + j], rep_r.at[3 + j], rep(xh, (y + j) % 4))

    for j in range(1, 4):
        rep_gather(j, y).start()

    use(2, 6)

    ag_z_wait(0, 4, 0)
    ag_z_wait(0, 4, 1)
    ag_b_send(0, 4)
    ag_z_wait(1, 4, 1)
    ag_b_send(1, 4)
    sib_copy(0, 4, c).start()
    ag_z_wait(1, 4, 2)
    to_sib_other(3)
    for o in (1, 7, 0):
        rs_b_send(o)

    for p in (2, 0):
        for way in (0, 1):
            rs_send(way, 1, p)
    for o in (3, 5):
        rs_x(o).wait_recv()
    for way in (0, 1):
        rs_send(way, 1, 1)

    ag_b_wait(0, 4)
    ag_b_wait(1, 4)
    sib_copy(1, 4, c).start()
    use(3, 5)

    for p in (2, 0):
        for way in (0, 1):
            rs_send(way, 2, p)
    for o in (2, 6):
        rs_x(o).wait_recv()
    for way in (0, 1):
        rs_send(way, 2, 1)

    use(4)
    valv[...] = acc[...].astype(BF16)
    outs = [pltpu.make_async_copy(valv, val_out, out_sem.at[0])]
    outs[0].start()

    for p in (2, 0):
        for way in (0, 1):
            rs_send(way, 3, p)
    for o in (1, 7):
        rs_x(o).wait_recv()
    for way in (0, 1):
        rs_send(way, 3, 1)

    loads[5].wait()
    for j in range(1, 4):
        rep_scatter(j).wait_send()
        rep_gather(j, (y + 4 - j) % 4).wait_recv()

    @pl.loop(0, SH // BLK)
    def _(i):
        at = pl.ds(pl.multiple_of(i * BLK, BLK), BLK)
        outer = tot[at, :] * 0.125
        new = 0.9 * momv[at, :] + outer
        rpv[at, :] = new
        diff[at, :] = opv[at, :] - 0.7 * (outer + 0.9 * new)

    for way in (0, 1):
        rs_z(way, 3, 2).wait_recv()
    summed(xq.at[8], ox, z, 0, HF, [zr.at[0, 3, 2], zr.at[1, 3, 2]])
    rs_x(8).start()

    def finish(start, received):
        @pl.loop(0, HF // BLK)
        def _(i):
            at = pl.multiple_of(i * BLK, BLK)
            dwv[pl.ds(pl.multiple_of(start + at, BLK), BLK), :] = total(x, z, start, at, received) * back

    rs_x(0).wait_recv()
    for way in (0, 1):
        rs_z(way, 3, 1).wait_recv()
    finish(HF, [xr.at[0], zr.at[0, 3, 1], zr.at[1, 3, 1]])
    for way in (0, 1):
        rs_z(way, 3, 0).wait_recv()
    rs_x(8).wait_recv()
    finish(0, [xr.at[8], zr.at[0, 3, 0], zr.at[1, 3, 0]])
    outs.append(pltpu.make_async_copy(dwv, dw_out.at[0], out_sem.at[1]))
    outs[1].start()

    for k in range(1, 5):
        for way in (0, 1):
            for p in (0, 1, 2):
                if k < 4 or p == 1 or (way, p) in ((0, 0), (1, 2)):
                    ag_z(way, k, p, far(way, k - 1)).wait_send()
                j = k - 1
                if j > 0 or p == 1 or (way, p) in ((0, 0), (1, 2)):
                    rs_z(way, j, p).wait_send()
    ag_x(0, x, z, 0, HF).wait_send()
    ag_x(1, x, z, HF, HF).wait_send()
    for k in range(1, 5):
        for way in (0, 1):
            n, start, size = b_of(way, k)
            ag_x(n, x, far(way, k), start, size).wait_send()
    for n in range(9):
        rs_x(n).wait_send()
    for xrel in (0, 1):
        for o in range(NZ):
            sib_copy(xrel, o, c).wait_send()
    tok_x.wait_send()
    tok_g.wait_send()
    for j in range(1, 4):
        rep_gather(j, y).wait_send()
    outs.append(pltpu.make_async_copy(diff, np_out, out_sem.at[2]))
    outs.append(pltpu.make_async_copy(rpv, nm_out, out_sem.at[3]))
    outs[2].start()
    outs[3].start()
    pltpu.make_async_copy(dxv, dx_out, dx_sem.at[0]).wait()
    for copy in outs:
        copy.wait()


def local(grad_scale, activations, cotangent, inner_weight, outer_params, replica_params, momentum):
    tokens, width = activations.shape
    kv = cotangent.shape[1]
    any_spec = pl.BlockSpec(memory_space=pl.ANY)
    dma = pltpu.SemaphoreType.DMA
    vm = pltpu.VMEM
    return pl.pallas_call(
        functools.partial(kernel, grad_scale),
        out_shape=(
            jax.ShapeDtypeStruct((tokens, kv), BF16),
            jax.ShapeDtypeStruct((tokens, width), BF16),
            jax.ShapeDtypeStruct((1, SH, kv), F32),
            jax.ShapeDtypeStruct((SH, kv), F32),
            jax.ShapeDtypeStruct((SH, kv), F32),
        ),
        in_specs=[any_spec] * 6,
        out_specs=(any_spec,) * 5,
        scratch_shapes=[
            vm((tokens, width), BF16),
            vm((2 * tokens, width // 2), BF16),
            vm((2 * tokens, kv), BF16),
            vm((16, 2 * SH, kv), BF16),
            vm((16, SH, kv), F32),
            vm((2, 4, 3, HF, kv), BF16),
            vm((2, 4, 3, HF, kv), BF16),
            vm((9, HF, kv), BF16),
            vm((9, HF, kv), BF16),
            vm((tokens, width), BF16),
            vm((tokens, kv), F32),
            vm((tokens, kv), BF16),
            vm((SH, kv), F32),
            vm((SH, kv), F32),
            vm((SH, kv), F32),
            vm((SH, kv), F32),
            vm((SH, kv), F32),
            vm((3, QT, kv), F32),
            vm((2, QT, kv), F32),
            vm((SH, kv), F32),
            vm((8, 128), F32),
            vm((8, 128), F32),
            vm((NZ - 1, 8, 128), F32),
            dma((6,)), dma((1,)), dma((4,)), dma((1,)),
            dma((2, 4, 3)), dma((2, 4, 3)), dma((10,)), dma((10,)),
            dma((16,)), dma((16,)), dma((2,)), dma((2,)),
            dma((2, 4, 3)), dma((2, 4, 3)), dma((9,)), dma((9,)),
            dma((8,)), dma((8,)), dma((7,)), dma((7,)),
        ],
        compiler_params=pltpu.CompilerParams(
            collective_id=0, has_side_effects=True, vmem_limit_bytes=56 << 20
        ),
        name="step",
    )(activations, cotangent, inner_weight, outer_params, replica_params, momentum)


def solution(mesh):
    rows = P(("replica", "fsdp"), None)
    placed = (rows, rows, P("replica", "fsdp", None), P("fsdp", None), P("replica", "fsdp", None), P("fsdp", None))

    def run(activations, *rest):
        grad_scale = 1.0 / math.sqrt(activations.shape[0] // mesh.shape["replica"])
        return jax.shard_map(
            functools.partial(local, grad_scale),
            mesh=mesh,
            in_specs=placed,
            out_specs=(rows, rows, P("replica", "fsdp", None), P("fsdp", None), P("fsdp", None)),
            check_vma=False,
        )(activations, *rest)

    return run
```

```python
import functools
import math

import jax
import jax.numpy as jnp
from jax import lax
from jax.experimental import pallas as pl
from jax.experimental.pallas import tpu as pltpu
from jax.sharding import PartitionSpec as P

MESH = pl.DeviceIdType.MESH
F32 = jnp.float32
BF16 = jnp.bfloat16

NZ = 8
SH = 128
HF = 64
QT = 32
BLK = 16


def encode(v):
    a = v * v
    b = a * a
    return (b * a * (v * jnp.abs(v))).astype(BF16)


def decode(q):
    t = q.astype(F32)
    a = lax.rsqrt(lax.rsqrt(jnp.maximum(jnp.abs(t), 1e-37)))
    r = a * lax.rsqrt(a)
    return jnp.where(t < 0, -r, r)


def kernel(
    grad_scale,
    x_in, g_in, w_in, op_in, rp_in, mom_in,
    val_out, dx_out, dw_out, np_out, nm_out,
    xv, xs, gs, W, part, zq, zr, xq, xr, acc,
    opv, rpv, momv, diff, ryv, xhv, tot, mine, mxr, pair, mzr,
    load_sem, xs_sem,
    agz_s, agz_r, agx_s, agx_r, sib_s, sib_r, tok_s, tok_r,
    rsz_s, rsz_r, rsx_s, rsx_r, mx_s, mx_r, rep_s, rep_r,
):
    r = lax.axis_index("replica")
    f = lax.axis_index("fsdp")
    xh, y = r // 4, r % 4
    x, z, c = f // 16, (f // 2) % NZ, f % 2
    ox, oc = 1 - x, 1 - c

    def zmod(v):
        return (v + 2 * NZ) % NZ

    def dev(xx, zz, cc):
        return (r, xx * 16 + zz * 2 + cc)

    def rep(hh, yy):
        return (hh * 4 + yy, f)

    def idx(xx, zz):
        return xx * NZ + zz

    x_nb, sib = dev(ox, z, c), dev(x, z, oc)
    z_nb = (dev(x, zmod(z + 1), c), dev(x, zmod(z - 1), c))
    xh_nb = rep(1 - xh, y)

    def remote(src, dst, ss, rs, to):
        return pltpu.make_async_remote_copy(
            src_ref=src, dst_ref=dst, send_sem=ss, recv_sem=rs, device_id=to, device_id_type=MESH
        )

    def cols(j, cc):
        return pl.ds(pl.multiple_of(j * 256 + cc * SH, SH), SH)

    loads = [
        pltpu.make_async_copy(w_in.at[0], W.at[idx(x, z), pl.ds(pl.multiple_of(c * SH, SH), SH)], load_sem.at[0]),
        pltpu.make_async_copy(op_in, opv, load_sem.at[1]),
        pltpu.make_async_copy(rp_in.at[0], rpv, load_sem.at[2]),
        pltpu.make_async_copy(g_in, gs.at[pl.ds(0, 384)], load_sem.at[3]),
        pltpu.make_async_copy(x_in, xv, load_sem.at[4]),
        pltpu.make_async_copy(mom_in, momv, load_sem.at[5]),
    ]
    for copy in loads[:4]:
        copy.start()

    barrier = pltpu.get_barrier_semaphore()
    peers = [x_nb, sib, xh_nb]
    peers += [dev(x, zmod(z + j), c) for j in range(1, NZ)]
    peers += [rep(xh, (y + j) % 4) for j in range(1, 4)]
    for peer in peers:
        pl.semaphore_signal(barrier, inc=1, device_id=peer, device_id_type=MESH)
    pl.semaphore_wait(barrier, len(peers))

    def rows(p, k=1, way=0):
        if p == 1:
            if k == 4:
                return HF + QT * way, QT
            return HF, HF
        return 0, HF

    def wpiece(xx, zz, start, size, cc=None):
        cc = c if cc is None else cc
        return W.at[idx(xx, zz), pl.ds(pl.multiple_of(cc * SH + start, QT), size)]

    def far(way, k):
        return zmod(z - k) if way == 0 else zmod(z + k)

    def ag_z(way, k, p, at):
        start, size = rows(p, k, way)
        ref = wpiece(ox if p == 2 else x, at, start, size)
        return remote(ref, ref, agz_s.at[way, k - 1, p], agz_r.at[way, k - 1, p], z_nb[way])

    def ag_z_send(way, k, p):
        ag_z(way, k, p, far(way, k - 1)).start()

    def ag_z_wait(way, k, p):
        ag_z(way, k, p, far(way, k)).wait_recv()

    def ag_x(n, xx, zz, start, size):
        ref = wpiece(xx, zz, start, size)
        return remote(ref, ref, agx_s.at[n], agx_r.at[n], x_nb)

    def b_of(way, k):
        if k == 4:
            return 8 + way, HF + QT * way, QT
        return 2 + way * 3 + k - 1, HF, HF

    def ag_b_send(way, k):
        n, start, size = b_of(way, k)
        ag_x(n, x, far(way, k), start, size).start()

    def ag_b_wait(way, k):
        n, start, size = b_of(way, k)
        ag_x(n, ox, far(way, k), start, size).wait_recv()

    def sib_copy(xrel, o, cc):
        ref = wpiece(x if xrel == 0 else ox, zmod(z + o), 0, SH, cc)
        n = xrel * NZ + o
        return remote(ref, ref, sib_s.at[n], sib_r.at[n], sib)

    loads[0].wait()
    own_a = wpiece(x, z, 0, HF)
    ag_x(0, x, z, 0, HF).start()
    for way in (0, 1):
        ag_z_send(way, 1, 0)
    ag_x(1, x, z, HF, HF).start()
    for way in (0, 1):
        ag_z_send(way, 1, 1)

    @pl.loop(0, 16)
    def _(j):
        at = pl.ds(pl.multiple_of(j * SH, SH), SH)
        remote(x_in.at[:, cols(j, oc)], xs.at[pl.ds(384, 384), at], tok_s.at[0], tok_r.at[0], sib).start()
        pltpu.make_async_copy(x_in.at[:, cols(j, c)], xs.at[pl.ds(0, 384), at], xs_sem.at[0]).start()

    tok_g = remote(g_in, gs.at[pl.ds(384, 384)], tok_s.at[1], tok_r.at[1], sib)
    tok_g.start()
    sib_copy(0, 0, c).start()
    loads[4].start()
    loads[5].start()

    loads[1].wait()
    loads[2].wait()

    @pl.loop(0, SH // BLK)
    def _(i):
        at = pl.ds(pl.multiple_of(i * BLK, BLK), BLK)
        diff[at, :] = opv[at, :] - rpv[at, :]

    def quarter(yy):
        return pl.ds(pl.multiple_of(yy * QT, QT), QT)

    def rep_scatter(j):
        to = (y + j) % 4
        return remote(diff.at[quarter(to)], ryv.at[j - 1], rep_s.at[j - 1], rep_r.at[j - 1], rep(xh, to))

    for j in range(1, 4):
        rep_scatter(j).start()

    def use(xrel, *offsets):
        for o in offsets:
            sib_copy(xrel, o, oc).wait_recv()
        first, step = offsets[0], offsets[-1] - offsets[0]

        @pl.loop(0, len(offsets))
        def _(t):
            i = idx(x if xrel == 0 else ox, zmod(z + first + t * step))
            at = pl.ds(pl.multiple_of(i * 256, 256), 256)
            w = W[i]
            dx_out[:, at] = lax.dot_general(
                gs[pl.ds(0, 384), :], w, (((1,), (1,)), ((), ())), preferred_element_type=F32
            ).astype(BF16)
            acc[...] += jnp.dot(xv[:, at], w, preferred_element_type=F32)

    acc[...] = jnp.zeros_like(acc)
    loads[3].wait()
    loads[4].wait()
    use(0, 0)

    ag_x(0, ox, z, 0, HF).wait_recv()
    for way in (0, 1):
        ag_z_send(way, 1, 2)

    tok_x = remote(xs.at[pl.ds(384, 384)], xs.at[pl.ds(384, 384)], tok_s.at[0], tok_r.at[0], sib)
    pltpu.make_async_copy(xs.at[pl.ds(0, 384)], xs.at[pl.ds(0, 384)], xs_sem.at[0]).wait()
    tok_g.wait_recv()
    tok_x.wait_recv()

    def partial(first, last):
        @pl.loop(first, last)
        def _(i):
            at = pl.ds(pl.multiple_of(i * 512, 512), 512)
            part[pl.ds(i * 4, 4)] = lax.dot_general(
                xs[:, at], gs[...], (((0,), (0,)), ((), ())), preferred_element_type=F32
            ).reshape(4, SH, 1024)

    def forward(k, p):
        for way in (0, 1):
            ag_z_wait(way, k, p)
            if k < 3 or p == 1 or (way, p) in ((0, 0), (1, 2)):
                ag_z_send(way, k + 1, p)
            if p == 1:
                ag_b_send(way, k)

    def off(way, k):
        return (NZ - k) % NZ if way == 0 else k

    def to_sib(k):
        for way in (0, 1):
            sib_copy(0, off(way, k), c).start()

    def to_sib_other(k):
        for way in (0, 1):
            ag_b_wait(way, k)
            sib_copy(1, off(way, k), c).start()

    partial(0, 1)
    forward(1, 0)
    partial(1, 2)
    forward(1, 1)
    to_sib(1)

    for j in range(1, 4):
        rep_scatter(j).wait_recv()
    tot[quarter(y), :] = ((diff[quarter(y), :] + ryv[0]) + ryv[1]) + ryv[2]
    xhv[0] = tot[quarter(y), :]
    rep_x = remote(xhv.at[0], xhv.at[1], rep_s.at[3], rep_r.at[3], xh_nb)
    rep_x.start()
    partial(2, 4)
    forward(1, 2)

    ag_x(1, ox, z, HF, HF).wait_recv()
    sib_copy(1, 0, c).start()

    def largest(i, m):
        v = jnp.abs(part[i // 2, pl.ds(pl.multiple_of((i % 2) * HF, HF), HF), :])
        for j in range(HF // 8):
            m = jnp.maximum(m, v[8 * j : 8 * j + 8])
        return m

    wide = lax.fori_loop(0, 32, largest, jnp.zeros((8, 1024), F32))
    narrow = wide[:, 0:128]
    for j in range(1, 8):
        narrow = jnp.maximum(narrow, wide[:, j * 128 : (j + 1) * 128])
    mine[...] = narrow
    max_x = remote(mine, mxr, mx_s.at[0], mx_r.at[0], x_nb)
    max_x.start()

    def tile(m):
        return jnp.maximum(jnp.full((8, 128), jnp.max(m), F32), 1e-30)

    own_scale = jnp.max(2048.0 / tile(mine[...]))

    def encoded(dst, xx, zz, start, size, factor, received):
        @pl.loop(0, size // BLK)
        def _(i):
            at = pl.multiple_of(i * BLK, BLK)
            dst[pl.ds(at, BLK), :] = encode(total(xx, zz, start, at, factor, received))

    def total(xx, zz, start, at, factor, received):
        v = part[idx(xx, zz), pl.ds(pl.multiple_of(start + at, BLK), BLK), :] * factor
        for ref, by in received:
            w = decode(ref[pl.ds(pl.multiple_of(at, BLK), BLK), :])
            v = v + (w if by is None else w * by)
        return v

    def rs_x(n):
        return remote(xq.at[n], xr.at[n], rsx_s.at[n], rsx_r.at[n], x_nb)

    def rs_b_send(o):
        encoded(xq.at[o], ox, zmod(z + o), HF, HF, own_scale, [])
        rs_x(o).start()

    def rs_z(way, j, p):
        size = QT if (j == 0 and p == 1) else HF
        at = QT * way if (j == 0 and p == 1) else 0
        here, there = zq.at[way, j, p, pl.ds(at, size)], zr.at[way, j, p, pl.ds(at, size)]
        return remote(here, there, rsz_s.at[way, j, p], rsz_r.at[way, j, p], z_nb[way])

    def rs_send(way, j, p):
        o = 4 - j if way == 0 else (4 + j) % NZ
        zz, col = zmod(z + o), (ox if p == 2 else x)
        out, crossed = zq.at[way, j, p], xr.at[o]
        if p != 1:
            if j > 0 and not (j == 1 and (way, p) in ((0, 2), (1, 0))):
                rs_z(way, j - 1, p).wait_recv()
                received = [(zr.at[way, j - 1, p], None)]
            else:
                received = []
            encoded(out, col, zz, 0, HF, scale, received)
        elif j >= 2:
            rs_z(way, j - 1, p).wait_recv()
            encoded(out, col, zz, HF, HF, scale, [(crossed, ratio), (zr.at[way, j - 1, p], None)])
        else:
            for half in (0, 1):
                at = pl.ds(QT * half, QT)
                if j == 0 and half == way:
                    encoded(out.at[at], col, zz, HF + QT * half, QT, scale, [(crossed.at[at], ratio)])
                elif j == 1 and half == way:
                    rs_z(way, 0, p).wait_recv()
                    encoded(
                        out.at[at], col, zz, HF + QT * half, QT, scale,
                        [(crossed.at[at], ratio), (zr.at[way, 0, p, at], None)],
                    )
                elif j == 1:
                    encoded(out.at[at], col, zz, HF + QT * half, QT, scale, [(crossed.at[at], ratio)])
        rs_z(way, j, p).start()

    for o in (4, 3, 5):
        rs_b_send(o)
    use(1, 0)

    max_x.wait()
    pair[...] = jnp.maximum(mine[...], mxr[...])

    def max_z(j):
        return remote(pair, mzr.at[j - 1], mx_s.at[j], mx_r.at[j], dev(x, zmod(z + j), c))

    for j in range(1, NZ):
        max_z(j).start()

    forward(2, 0)
    use(0, 1, 7)
    forward(2, 1)
    to_sib(2)
    to_sib_other(1)
    forward(2, 2)

    for j in range(1, NZ):
        max_z(j).wait()
    most = pair[...]
    for j in range(NZ - 1):
        most = jnp.maximum(most, mzr[j])
    top = tile(most)
    scale = jnp.max(2048.0 / top)
    back = jnp.max(top * (grad_scale / 2048.0))
    ratio = jnp.max(tile(mxr[...]) / top)

    use(1, 1, 7)
    forward(3, 0)
    use(0, 2, 6)
    forward(3, 1)
    to_sib(3)
    forward(3, 2)

    rs_send(0, 0, 0)
    rs_send(1, 0, 2)
    rs_x(4).wait_recv()
    rs_send(0, 0, 1)
    rs_send(1, 0, 1)
    rs_send(0, 1, 2)
    rs_send(1, 1, 0)
    for o in (2, 6):
        rs_b_send(o)

    rep_x.wait()
    tot[quarter(y), :] = xhv[0] + xhv[1]

    def rep_gather(j, at):
        ref = tot.at[quarter(at)]
        return remote(ref, ref, rep_s.at[3 + j], rep_r.at[3 + j], rep(xh, (y + j) % 4))

    for j in range(1, 4):
        rep_gather(j, y).start()

    use(0, 3, 5)

    ag_z_wait(0, 4, 1)
    ag_b_send(0, 4)
    ag_z_wait(1, 4, 1)
    ag_b_send(1, 4)
    ag_z_wait(0, 4, 0)
    sib_copy(0, 4, c).start()
    ag_z_wait(1, 4, 2)
    to_sib_other(2)

    rs_send(0, 1, 0)
    rs_send(1, 1, 2)
    for o in (3, 5):
        rs_x(o).wait_recv()
    for way in (0, 1):
        rs_send(way, 1, 1)
    for o in (1, 7, 0):
        rs_b_send(o)
    use(1, 2, 6)
    use(0, 4)

    rs_send(0, 2, 2)
    rs_send(1, 2, 0)
    to_sib_other(3)
    rs_send(0, 2, 0)
    rs_send(1, 2, 2)
    use(1, 3, 5)
    for o in (2, 6):
        rs_x(o).wait_recv()
    for way in (0, 1):
        rs_send(way, 2, 1)

    ag_b_wait(0, 4)
    ag_b_wait(1, 4)
    sib_copy(1, 4, c).start()

    loads[5].wait()
    for j in range(1, 4):
        rep_gather(j, (y + 4 - j) % 4).wait_recv()

    @pl.loop(0, SH // BLK)
    def _(i):
        at = pl.ds(pl.multiple_of(i * BLK, BLK), BLK)
        outer = tot[at, :] * 0.125
        new = 0.9 * momv[at, :] + outer
        nm_out[at, :] = new
        np_out[at, :] = opv[at, :] - 0.7 * (outer + 0.9 * new)

    rs_send(0, 3, 2)
    rs_send(1, 3, 2)
    use(1, 4)
    val_out[...] = acc[...].astype(BF16)
    rs_send(0, 3, 0)
    rs_send(1, 3, 0)
    for o in (1, 7):
        rs_x(o).wait_recv()
    for way in (0, 1):
        rs_send(way, 3, 1)

    for way in (0, 1):
        rs_z(way, 3, 2).wait_recv()
    encoded(xq.at[8], ox, z, 0, HF, scale, [(zr.at[0, 3, 2], None), (zr.at[1, 3, 2], None)])
    rs_x(8).start()

    def finish(start, received):
        @pl.loop(0, HF // BLK)
        def _(i):
            at = pl.multiple_of(i * BLK, BLK)
            dw_out[0, pl.ds(pl.multiple_of(start + at, BLK), BLK), :] = (
                total(x, z, start, at, scale, received) * back
            )

    rs_x(8).wait_recv()
    for way in (0, 1):
        rs_z(way, 3, 0).wait_recv()
    finish(0, [(xr.at[8], None), (zr.at[0, 3, 0], None), (zr.at[1, 3, 0], None)])
    rs_x(0).wait_recv()
    for way in (0, 1):
        rs_z(way, 3, 1).wait_recv()
    finish(HF, [(xr.at[0], ratio), (zr.at[0, 3, 1], None), (zr.at[1, 3, 1], None)])

    for k in range(1, 5):
        for way in (0, 1):
            for p in (0, 1, 2):
                if k < 4 or p == 1 or (way, p) in ((0, 0), (1, 2)):
                    ag_z(way, k, p, far(way, k - 1)).wait_send()
                j = k - 1
                if j > 0 or p == 1 or (way, p) in ((0, 0), (1, 2)):
                    rs_z(way, j, p).wait_send()
    ag_x(0, x, z, 0, HF).wait_send()
    ag_x(1, x, z, HF, HF).wait_send()
    for k in range(1, 5):
        for way in (0, 1):
            n, start, size = b_of(way, k)
            ag_x(n, x, far(way, k), start, size).wait_send()
    for n in range(9):
        rs_x(n).wait_send()
    for xrel in (0, 1):
        for o in range(NZ):
            sib_copy(xrel, o, c).wait_send()
    tok_x.wait_send()
    tok_g.wait_send()
    for j in range(1, 4):
        rep_scatter(j).wait_send()
        rep_gather(j, y).wait_send()


def store(*refs):
    copies = [pltpu.make_async_copy(refs[i], refs[5 + i], refs[10].at[i]) for i in range(5)]
    for copy in copies:
        copy.start()
    for copy in copies:
        copy.wait()


def local(grad_scale, activations, cotangent, inner_weight, outer_params, replica_params, momentum):
    tokens, width = activations.shape
    kv = cotangent.shape[1]
    any_spec = pl.BlockSpec(memory_space=pl.ANY)
    vmem_spec = pl.BlockSpec(memory_space=pltpu.VMEM)
    dma = pltpu.SemaphoreType.DMA
    vm = pltpu.VMEM
    results = pl.pallas_call(
        functools.partial(kernel, grad_scale),
        out_shape=(
            vm((tokens, kv), BF16),
            vm((tokens, width), BF16),
            vm((1, SH, kv), F32),
            vm((SH, kv), F32),
            vm((SH, kv), F32),
        ),
        in_specs=[any_spec] * 6,
        out_specs=(vmem_spec,) * 5,
        scratch_shapes=[
            vm((tokens, width), BF16),
            vm((2 * tokens, width // 2), BF16),
            vm((2 * tokens, kv), BF16),
            vm((16, 2 * SH, kv), BF16),
            vm((16, SH, kv), F32),
            vm((2, 4, 3, HF, kv), BF16),
            vm((2, 4, 3, HF, kv), BF16),
            vm((9, HF, kv), BF16),
            vm((9, HF, kv), BF16),
            vm((tokens, kv), F32),
            vm((SH, kv), F32),
            vm((SH, kv), F32),
            vm((SH, kv), F32),
            vm((SH, kv), F32),
            vm((3, QT, kv), F32),
            vm((2, QT, kv), F32),
            vm((SH, kv), F32),
            vm((8, 128), F32),
            vm((8, 128), F32),
            vm((8, 128), F32),
            vm((NZ - 1, 8, 128), F32),
            dma((6,)), dma((1,)),
            dma((2, 4, 3)), dma((2, 4, 3)), dma((10,)), dma((10,)),
            dma((16,)), dma((16,)), dma((2,)), dma((2,)),
            dma((2, 4, 3)), dma((2, 4, 3)), dma((9,)), dma((9,)),
            dma((8,)), dma((8,)), dma((7,)), dma((7,)),
        ],
        compiler_params=pltpu.CompilerParams(
            collective_id=0, has_side_effects=True, vmem_limit_bytes=57 << 20
        ),
        name="step",
    )(activations, cotangent, inner_weight, outer_params, replica_params, momentum)
    return pl.pallas_call(
        store,
        out_shape=[jax.ShapeDtypeStruct(v.shape, v.dtype) for v in results],
        in_specs=[vmem_spec] * 5,
        out_specs=[pl.BlockSpec(memory_space=pltpu.HBM)] * 5,
        scratch_shapes=[dma((5,))],
        compiler_params=pltpu.CompilerParams(vmem_limit_bytes=1 << 20),
        name="store",
    )(*[pltpu.with_memory_space_constraint(v, pltpu.VMEM) for v in results])


def solution(mesh):
    rows = P(("replica", "fsdp"), None)
    placed = (rows, rows, P("replica", "fsdp", None), P("fsdp", None), P("replica", "fsdp", None), P("fsdp", None))

    def run(activations, *rest):
        grad_scale = 1.0 / math.sqrt(activations.shape[0] // mesh.shape["replica"])
        return jax.shard_map(
            functools.partial(local, grad_scale),
            mesh=mesh,
            in_specs=placed,
            out_specs=(rows, rows, P("replica", "fsdp", None), P("fsdp", None), P("fsdp", None)),
            check_vma=False,
        )(activations, *rest)

    return run
```

```python
import functools
import math

import jax
import jax.numpy as jnp
from jax import lax
from jax.experimental import pallas as pl
from jax.experimental.pallas import tpu as pltpu
from jax.sharding import PartitionSpec as P

MESH = pl.DeviceIdType.MESH
F32 = jnp.float32
BF16 = jnp.bfloat16

NZ = 8
SH = 128
HF = 64
QT = 32
BLK = 16


def encode(v):
    a = v * v
    b = a * a
    return (b * a * (v * jnp.abs(v))).astype(BF16)


def decode(q):
    t = q.astype(F32)
    a = lax.rsqrt(lax.rsqrt(jnp.maximum(jnp.abs(t), 1e-37)))
    r = a * lax.rsqrt(a)
    return jnp.where(t < 0, -r, r)


def kernel(
    grad_scale,
    x_in, g_in, w_in, op_in, rp_in, mom_in,
    val_out, dx_out, dw_out, np_out, nm_out,
    xv, xs, gs, W, part, zq, zr, xq, xr, acc,
    opv, rpv, momv, diff, ryv, xhv, tot, tq, tr,
    load_sem, xs_sem, tok_s, tok_r, link_s, sib_s, top_s, rep_s,
    agz_r, agx_r, sib_r, rsz_r, rsx_r, top_r, rep_r,
):
    r = lax.axis_index("replica")
    f = lax.axis_index("fsdp")
    xh, y = r // 4, r % 4
    x, z, c = f // 16, (f // 2) % NZ, f % 2
    ox, oc = 1 - x, 1 - c

    def zmod(v):
        return (v + 2 * NZ) % NZ

    def dev(xx, zz, cc):
        return (r, xx * 16 + zz * 2 + cc)

    def rep(hh, yy):
        return (hh * 4 + yy, f)

    def idx(xx, zz):
        return xx * NZ + zz

    x_nb, sib = dev(ox, z, c), dev(x, z, oc)
    z_nb = (dev(x, zmod(z + 1), c), dev(x, zmod(z - 1), c))
    xh_nb = rep(1 - xh, y)

    def remote(src, dst, ss, rs, to):
        return pltpu.make_async_remote_copy(
            src_ref=src, dst_ref=dst, send_sem=ss, recv_sem=rs, device_id=to, device_id_type=MESH
        )

    def cols(j, cc):
        return pl.ds(pl.multiple_of(j * 256 + cc * SH, SH), SH)

    loads = [
        pltpu.make_async_copy(w_in.at[0], W.at[idx(x, z), pl.ds(pl.multiple_of(c * SH, SH), SH)], load_sem.at[0]),
        pltpu.make_async_copy(op_in, opv, load_sem.at[1]),
        pltpu.make_async_copy(rp_in.at[0], rpv, load_sem.at[2]),
        pltpu.make_async_copy(g_in, gs.at[pl.ds(0, 384)], load_sem.at[3]),
        pltpu.make_async_copy(x_in, xv, load_sem.at[4]),
        pltpu.make_async_copy(mom_in, momv, load_sem.at[5]),
    ]
    for copy in loads[:4]:
        copy.start()

    barrier = pltpu.get_barrier_semaphore()
    peers = [sib, x_nb, xh_nb, *z_nb]
    peers += [rep(xh, (y + j) % 4) for j in range(1, 4)]
    for peer in peers:
        pl.semaphore_signal(barrier, inc=1, device_id=peer, device_id_type=MESH)
    pl.semaphore_wait(barrier, len(peers))

    def rows(p, k=1, way=0):
        if p == 1:
            if k == 4:
                return HF + QT * way, QT
            return HF, HF
        return 0, HF

    def wpiece(xx, zz, start, size, cc=None):
        cc = c if cc is None else cc
        return W.at[idx(xx, zz), pl.ds(pl.multiple_of(cc * SH + start, QT), size)]

    def far(way, k):
        return zmod(z - k) if way == 0 else zmod(z + k)

    def ag_z(way, k, p, at):
        start, size = rows(p, k, way)
        ref = wpiece(ox if p == 2 else x, at, start, size)
        return remote(ref, ref, link_s.at[0], agz_r.at[way, k - 1, p], z_nb[way])

    def ag_z_send(way, k, p):
        ag_z(way, k, p, far(way, k - 1)).start()

    def ag_z_wait(way, k, p):
        ag_z(way, k, p, far(way, k)).wait_recv()

    def ag_x(n, zz, start, size):
        ref = wpiece(x, zz, start, size)
        return remote(ref, ref, link_s.at[0], agx_r.at[n], x_nb)

    def ag_x_wait(n, zz, start, size):
        ref = wpiece(ox, zz, start, size)
        remote(ref, ref, link_s.at[0], agx_r.at[n], x_nb).wait_recv()

    def ag_b_send(way, k):
        start, size = rows(1, k, way)
        ag_x(1 + k, far(way, k), start, size).start()

    def ag_b_wait(k):
        ag_x_wait(1 + k, far(0, k), 0 if k < 4 else HF, SH if k < 4 else HF)

    def sib_copy(xrel, o, cc):
        ref = wpiece(x if xrel == 0 else ox, zmod(z + o), 0, SH, cc)
        n = xrel * 5 + min(o, NZ - o)
        return remote(ref, ref, sib_s.at[0], sib_r.at[n], sib)

    def sib_wait(xrel, offsets):
        if len(offsets) == 1:
            sib_copy(xrel, offsets[0], oc).wait_recv()
        else:
            ref = W.at[idx(x if xrel == 0 else ox, zmod(z + offsets[0]))]
            remote(ref, ref, sib_s.at[0], sib_r.at[xrel * 5 + offsets[0]], sib).wait_recv()

    loads[0].wait()
    ag_x(0, z, 0, HF).start()
    for way in (0, 1):
        ag_z_send(way, 1, 0)
    for way in (0, 1):
        ag_z_send(way, 1, 1)

    @pl.loop(0, 16)
    def _(j):
        at = pl.ds(pl.multiple_of(j * SH, SH), SH)
        remote(x_in.at[:, cols(j, oc)], xs.at[pl.ds(384, 384), at], tok_s.at[0], tok_r.at[0], sib).start()
        pltpu.make_async_copy(x_in.at[:, cols(j, c)], xs.at[pl.ds(0, 384), at], xs_sem.at[0]).start()

    tok_g = remote(g_in, gs.at[pl.ds(384, 384)], tok_s.at[1], tok_r.at[1], sib)
    tok_g.start()
    sib_copy(0, 0, c).start()
    loads[4].start()
    loads[5].start()

    loads[1].wait()
    loads[2].wait()

    @pl.loop(0, SH // BLK)
    def _(i):
        at = pl.ds(pl.multiple_of(i * BLK, BLK), BLK)
        diff[at, :] = opv[at, :] - rpv[at, :]

    def quarter(yy):
        return pl.ds(pl.multiple_of(yy * QT, QT), QT)

    def rep_scatter(j):
        to = (y + j) % 4
        return remote(diff.at[quarter(to)], ryv.at[j - 1], rep_s.at[0], rep_r.at[0], rep(xh, to))

    for j in range(1, 4):
        rep_scatter(j).start()

    def use(xrel, *offsets):
        sib_wait(xrel, offsets)
        first, step = offsets[0], offsets[-1] - offsets[0]

        @pl.loop(0, len(offsets))
        def _(t):
            i = idx(x if xrel == 0 else ox, zmod(z + first + t * step))
            at = pl.ds(pl.multiple_of(i * 256, 256), 256)
            w = W[i]
            dx_out[:, at] = lax.dot_general(
                gs[pl.ds(0, 384), :], w, (((1,), (1,)), ((), ())), preferred_element_type=F32
            ).astype(BF16)
            acc[...] += jnp.dot(xv[:, at], w, preferred_element_type=F32)

    acc[...] = jnp.zeros_like(acc)
    loads[3].wait()
    loads[4].wait()
    use(0, 0)

    ag_x_wait(0, z, 0, HF)
    for way in (0, 1):
        ag_z_send(way, 1, 2)
    ag_x(1, z, HF, HF).start()

    tok_x = remote(xs.at[pl.ds(384, 384)], xs.at[pl.ds(384, 384)], tok_s.at[0], tok_r.at[0], sib)
    pltpu.make_async_copy(xs.at[pl.ds(0, 384)], xs.at[pl.ds(0, 384)], xs_sem.at[0]).wait()
    tok_g.wait_recv()
    tok_x.wait_recv()

    def partial(first, last):
        @pl.loop(first, last)
        def _(i):
            at = pl.ds(pl.multiple_of(i * 512, 512), 512)
            part[pl.ds(i * 4, 4)] = lax.dot_general(
                xs[:, at], gs[...], (((0,), (0,)), ((), ())), preferred_element_type=F32
            ).reshape(4, SH, 1024)

    def forward(k, p):
        for way in (0, 1):
            ag_z_wait(way, k, p)
            if k < 3:
                ag_z_send(way, k + 1, p)
            if p == 1:
                ag_b_send(way, k)

    def off(way, k):
        return (NZ - k) % NZ if way == 0 else k

    def to_sib(k):
        for way in (0, 1):
            sib_copy(0, off(way, k), c).start()

    def to_sib_other(k):
        ag_b_wait(k)
        for way in (0, 1):
            sib_copy(1, off(way, k), c).start()

    partial(0, 1)
    forward(1, 0)
    partial(1, 2)
    forward(1, 1)
    to_sib(1)

    remote(ryv, ryv, rep_s.at[0], rep_r.at[0], xh_nb).wait_recv()
    tot[quarter(y), :] = ((diff[quarter(y), :] + ryv[0]) + ryv[1]) + ryv[2]
    xhv[0] = tot[quarter(y), :]
    rep_x = remote(xhv.at[0], xhv.at[1], rep_s.at[0], rep_r.at[1], xh_nb)
    rep_x.start()
    partial(2, 4)
    forward(1, 2)

    ag_x_wait(1, z, HF, HF)
    sib_copy(1, 0, c).start()

    def largest(i, m):
        v = jnp.abs(part[i // 2, pl.ds(pl.multiple_of((i % 2) * HF, HF), HF), :])
        for j in range(HF // 8):
            m = jnp.maximum(m, v[8 * j : 8 * j + 8])
        return m

    wide = lax.fori_loop(0, 32, largest, jnp.zeros((8, 1024), F32))
    narrow = wide[:, 0:128]
    for j in range(1, 8):
        narrow = jnp.maximum(narrow, wide[:, j * 128 : (j + 1) * 128])

    def top_copy(n, to):
        return remote(tq.at[n], tr.at[n], top_s.at[0], top_r.at[n], to)

    tq[8] = narrow
    top_copy(8, x_nb).start()

    def tile(m):
        return jnp.maximum(jnp.full((8, 128), jnp.max(m), F32), 1e-30)

    own_scale = jnp.max(2048.0 / tile(narrow))

    def encoded(dst, xx, zz, start, size, factor, received):
        @pl.loop(0, size // BLK)
        def _(i):
            at = pl.multiple_of(i * BLK, BLK)
            dst[pl.ds(at, BLK), :] = encode(total(xx, zz, start, at, factor, received))

    def total(xx, zz, start, at, factor, received):
        v = part[idx(xx, zz), pl.ds(pl.multiple_of(start + at, BLK), BLK), :] * factor
        for ref, by in received:
            w = decode(ref[pl.ds(pl.multiple_of(at, BLK), BLK), :])
            v = v + w * by
        return v

    def rs_x(n):
        return remote(xq.at[n], xr.at[n], link_s.at[0], rsx_r.at[n if n < 5 else NZ - n if n < NZ else 5], x_nb)

    def rs_x_wait(o):
        ref = xr.at[o] if o in (0, 4, 8) else xr.at[pl.ds(0, 2)]
        remote(ref, ref, link_s.at[0], rsx_r.at[o if o < 5 else 5], x_nb).wait_recv()

    def rs_b_send(o):
        encoded(xq.at[o], ox, zmod(z + o), HF, HF, own_scale, [])
        rs_x(o).start()

    def rs_z(way, j, p):
        size = QT if (j == 0 and p == 1) else HF
        at = QT * way if (j == 0 and p == 1) else 0
        here, there = zq.at[way, j, p, pl.ds(at, size)], zr.at[way, j, p, pl.ds(at, size)]
        return remote(here, there, link_s.at[0], rsz_r.at[way, j, p], z_nb[way])

    factors = {}

    def prepare(way, j):
        top, came = jnp.maximum(tq[8], tr[8]), None
        if j > 0:
            top_copy(way * 4 + j - 1, z_nb[way]).wait_recv()
            came = tr[way * 4 + j - 1]
            top = jnp.maximum(top, came)
        tq[way * 4 + j] = top
        top_copy(way * 4 + j, z_nb[way]).start()
        whole = tile(top)
        factors[way, j] = (
            jnp.max(2048.0 / whole),
            jnp.max(tile(tr[8]) / whole),
            None if came is None else jnp.max(tile(came) / whole),
        )

    def rs_send(way, j, p):
        o = 4 - j if way == 0 else (4 + j) % NZ
        zz, col = zmod(z + o), (ox if p == 2 else x)
        out, crossed = zq.at[way, j, p], xr.at[o]
        scale, by_x, by_z = factors[way, j]
        if p != 1:
            received = []
            if j > 0 and not (j == 1 and (way, p) in ((0, 2), (1, 0))):
                rs_z(way, j - 1, p).wait_recv()
                received = [(zr.at[way, j - 1, p], by_z)]
            encoded(out, col, zz, 0, HF, scale, received)
        elif j >= 2:
            rs_z(way, j - 1, p).wait_recv()
            encoded(out, col, zz, HF, HF, scale, [(crossed, by_x), (zr.at[way, j - 1, p], by_z)])
        else:
            for half in (0, 1):
                at = pl.ds(QT * half, QT)
                received = [(crossed.at[at], by_x)]
                if j == 1 and half == way:
                    rs_z(way, 0, p).wait_recv()
                    received.append((zr.at[way, 0, p, at], by_z))
                if j == 1 or half == way:
                    encoded(out.at[at], col, zz, HF + QT * half, QT, scale, received)
        rs_z(way, j, p).start()

    for o in (4, 3, 5):
        rs_b_send(o)
    use(1, 0)
    forward(2, 0)
    use(0, 1, 7)
    forward(2, 1)
    to_sib(2)
    top_copy(8, x_nb).wait_recv()
    for way in (0, 1):
        prepare(way, 0)
    rs_send(0, 0, 0)
    rs_send(1, 0, 2)
    to_sib_other(1)
    forward(2, 2)
    rs_x_wait(4)
    rs_send(0, 0, 1)
    rs_send(1, 0, 1)
    use(1, 1, 7)
    for way in (0, 1):
        prepare(way, 1)
    rs_send(0, 1, 2)
    rs_send(1, 1, 0)
    for o in (2, 6):
        rs_b_send(o)
    use(0, 2, 6)

    rep_x.wait_recv()
    tot[quarter(y), :] = xhv[0] + xhv[1]

    def rep_gather(j, at):
        ref = tot.at[quarter(at)]
        return remote(ref, ref, rep_s.at[0], rep_r.at[2], rep(xh, (y + j) % 4))

    for j in range(1, 4):
        rep_gather(j, y).start()

    rs_send(0, 1, 0)
    rs_send(1, 1, 2)
    rs_x_wait(3)
    for way in (0, 1):
        rs_send(way, 1, 1)
    forward(3, 0)
    to_sib_other(2)
    forward(3, 1)
    to_sib(3)
    use(1, 2, 6)
    forward(3, 2)
    for way in (0, 1):
        prepare(way, 2)
    rs_send(0, 2, 2)
    rs_send(1, 2, 0)
    for o in (1, 7, 0):
        rs_b_send(o)
    rs_send(0, 2, 0)
    rs_send(1, 2, 2)
    use(0, 3, 5)
    rs_x_wait(2)
    for way in (0, 1):
        rs_send(way, 2, 1)

    ag_z_send(0, 4, 1)
    ag_z_send(1, 4, 1)
    ag_z_send(0, 4, 0)
    ag_z_send(1, 4, 2)
    for way in (0, 1):
        prepare(way, 3)
    rs_send(0, 3, 2)
    rs_send(1, 3, 2)
    to_sib_other(3)
    rs_send(0, 3, 0)
    rs_send(1, 3, 0)
    use(1, 3, 5)
    rs_x_wait(1)
    for way in (0, 1):
        rs_send(way, 3, 1)
    for way in (0, 1):
        ag_z_wait(way, 4, 1)
        ag_b_send(way, 4)
    ag_z_wait(0, 4, 0)
    sib_copy(0, 4, c).start()
    ag_z_wait(1, 4, 2)
    use(0, 4)
    ag_b_wait(4)
    sib_copy(1, 4, c).start()

    loads[5].wait()
    remote(ryv, ryv, rep_s.at[0], rep_r.at[2], xh_nb).wait_recv()

    @pl.loop(0, SH // BLK)
    def _(i):
        at = pl.ds(pl.multiple_of(i * BLK, BLK), BLK)
        outer = tot[at, :] * 0.125
        new = 0.9 * momv[at, :] + outer
        nm_out[at, :] = new
        np_out[at, :] = opv[at, :] - 0.7 * (outer + 0.9 * new)

    last = jnp.maximum(tq[8], tr[8])
    for way in (0, 1):
        top_copy(way * 4 + 3, z_nb[way]).wait_recv()
        last = jnp.maximum(last, tr[way * 4 + 3])
    tq[9] = last
    top_copy(9, x_nb).start()
    whole = tile(last)
    by_way = [jnp.max(tile(tr[way * 4 + 3]) / whole) for way in (0, 1)]
    for way in (0, 1):
        rs_z(way, 3, 2).wait_recv()
    encoded(xq.at[8], ox, z, 0, HF, jnp.max(2048.0 / whole), [(zr.at[way, 3, 2], by_way[way]) for way in (0, 1)])
    rs_x(8).start()
    use(1, 4)
    val_out[...] = acc[...].astype(BF16)

    def finish(start, received, add):
        @pl.loop(0, HF // BLK)
        def _(i):
            at = pl.multiple_of(i * BLK, BLK)
            out = pl.ds(pl.multiple_of(start + at, BLK), BLK)
            v = dw_out[0, out, :] if add else part[idx(x, z), out, :] * grad_scale
            for ref, by in received:
                v = v + decode(ref[pl.ds(at, BLK), :]) * by
            dw_out[0, out, :] = v

    def back(n):
        return jnp.max(tile(tr[n]) * (grad_scale / 2048.0))

    back_z = [back(way * 4 + 3) for way in (0, 1)]
    rs_x_wait(0)
    finish(HF, [(xr.at[0], back(8))], False)
    for way in (0, 1):
        rs_z(way, 3, 0).wait_recv()
    finish(0, [(zr.at[way, 3, 0], back_z[way]) for way in (0, 1)], False)
    top_copy(9, x_nb).wait_recv()
    back_x = back(9)
    for way in (0, 1):
        rs_z(way, 3, 1).wait_recv()
    finish(HF, [(zr.at[way, 3, 1], back_z[way]) for way in (0, 1)], True)
    rs_x_wait(8)
    finish(0, [(xr.at[8], back_x)], True)

    pieces = W.at[pl.ds(0, 15)]
    remote(pieces, pieces, link_s.at[0], top_r.at[0], x_nb).wait_send()
    pieces = W.at[pl.ds(0, 8)]
    remote(pieces, pieces, sib_s.at[0], top_r.at[0], sib).wait_send()
    tok_x.wait_send()
    tok_g.wait_send()
    remote(tr, tr, top_s.at[0], top_r.at[0], x_nb).wait_send()
    pieces = part.at[pl.ds(0, 7), pl.ds(0, QT)]
    remote(pieces, pieces, rep_s.at[0], top_r.at[0], xh_nb).wait_send()


def store(*refs):
    sems = refs[10]
    copies = [pltpu.make_async_copy(refs[i], refs[5 + i], sems.at[i]) for i in (0, 2, 3, 4)]
    step = refs[1].shape[0] // 4
    for n in range(4):
        at = pl.ds(n * step, step)
        copies.insert(0, pltpu.make_async_copy(refs[1].at[at], refs[6].at[at], sems.at[5 + n]))
    for copy in copies:
        copy.start()
    for copy in copies:
        copy.wait()


def local(grad_scale, activations, cotangent, inner_weight, outer_params, replica_params, momentum):
    tokens, width = activations.shape
    kv = cotangent.shape[1]
    any_spec = pl.BlockSpec(memory_space=pl.ANY)
    vmem_spec = pl.BlockSpec(memory_space=pltpu.VMEM)
    dma = pltpu.SemaphoreType.DMA
    vm = pltpu.VMEM
    results = pl.pallas_call(
        functools.partial(kernel, grad_scale),
        out_shape=(
            vm((tokens, kv), BF16),
            vm((tokens, width), BF16),
            vm((1, SH, kv), F32),
            vm((SH, kv), F32),
            vm((SH, kv), F32),
        ),
        in_specs=[any_spec] * 6,
        out_specs=(vmem_spec,) * 5,
        scratch_shapes=[
            vm((tokens, width), BF16),
            vm((2 * tokens, width // 2), BF16),
            vm((2 * tokens, kv), BF16),
            vm((16, 2 * SH, kv), BF16),
            vm((16, SH, kv), F32),
            vm((2, 4, 3, HF, kv), BF16),
            vm((2, 4, 3, HF, kv), BF16),
            vm((9, HF, kv), BF16),
            vm((9, HF, kv), BF16),
            vm((tokens, kv), F32),
            vm((SH, kv), F32),
            vm((SH, kv), F32),
            vm((SH, kv), F32),
            vm((SH, kv), F32),
            vm((3, QT, kv), F32),
            vm((2, QT, kv), F32),
            vm((SH, kv), F32),
            vm((10, 8, 128), F32),
            vm((10, 8, 128), F32),
            dma((6,)), dma((1,)), dma((2,)), dma((2,)),
            dma((1,)), dma((1,)), dma((1,)), dma((1,)),
            dma((2, 4, 3)), dma((6,)), dma((10,)), dma((2, 4, 3)), dma((6,)), dma((10,)), dma((3,)),
        ],
        compiler_params=pltpu.CompilerParams(
            collective_id=0, has_side_effects=True, vmem_limit_bytes=57 << 20
        ),
        name="step",
    )(activations, cotangent, inner_weight, outer_params, replica_params, momentum)
    return pl.pallas_call(
        store,
        out_shape=[jax.ShapeDtypeStruct(v.shape, v.dtype) for v in results],
        in_specs=[vmem_spec] * 5,
        out_specs=[pl.BlockSpec(memory_space=pltpu.HBM)] * 5,
        scratch_shapes=[dma((9,))],
        compiler_params=pltpu.CompilerParams(vmem_limit_bytes=1 << 20),
        name="store",
    )(*[pltpu.with_memory_space_constraint(v, pltpu.VMEM) for v in results])


def solution(mesh):
    rows = P(("replica", "fsdp"), None)
    placed = (rows, rows, P("replica", "fsdp", None), P("fsdp", None), P("replica", "fsdp", None), P("fsdp", None))

    def run(activations, *rest):
        grad_scale = 1.0 / math.sqrt(activations.shape[0] // mesh.shape["replica"])
        return jax.shard_map(
            functools.partial(local, grad_scale),
            mesh=mesh,
            in_specs=placed,
            out_specs=(rows, rows, P("replica", "fsdp", None), P("fsdp", None), P("fsdp", None)),
            check_vma=False,
        )(activations, *rest)

    return run
```

```python
import functools
import math

import jax
import jax.numpy as jnp
from jax import lax
from jax.experimental import pallas as pl
from jax.experimental.pallas import tpu as pltpu
from jax.sharding import PartitionSpec as P

MESH = pl.DeviceIdType.MESH
F32 = jnp.float32
BF16 = jnp.bfloat16

NZ = 8
LOW = 48
SH = 128
HF = 64
QT = 32
FIRST = ((0, 0), (1, 2), (1, 1))
BLK = 16


def encode(v):
    a = v * v
    b = a * a
    return (b * a * (v * jnp.abs(v))).astype(BF16)


def decode(q):
    t = q.astype(F32)
    a = lax.rsqrt(lax.rsqrt(jnp.maximum(jnp.abs(t), 1e-37)))
    r = a * lax.rsqrt(a)
    return jnp.where(t < 0, -r, r)


def kernel(
    grad_scale,
    x_in, g_in, w_in, op_in, rp_in, mom_in,
    val_out, dx_out, dw_out, np_out, nm_out,
    xv, xs, gs, W, part, zq, zr, xq, xr, acc,
    opv, rpv, momv, diff, ryv, xhv, tot, tq, tr,
    load_sem, xs_sem, tok_s, tok_r, link_s, sib_s, top_s, rep_s,
    agz_r, agx_r, sib_r, rsz_r, rsx_r, top_r, rep_r,
):
    r = lax.axis_index("replica")
    f = lax.axis_index("fsdp")
    xh, y = r // 4, r % 4
    x, z, c = f // 16, (f // 2) % NZ, f % 2
    ox, oc = 1 - x, 1 - c

    def zmod(v):
        return (v + 2 * NZ) % NZ

    def dev(xx, zz, cc):
        return (r, xx * 16 + zz * 2 + cc)

    def rep(hh, yy):
        return (hh * 4 + yy, f)

    def idx(xx, zz):
        return xx * NZ + zz

    x_nb, sib = dev(ox, z, c), dev(x, z, oc)
    z_nb = (dev(x, zmod(z + 1), c), dev(x, zmod(z - 1), c))
    outer = ((1 - xh) * 4 + y, ox * 16 + z * 2 + c)

    def remote(src, dst, ss, rs, to):
        return pltpu.make_async_remote_copy(
            src_ref=src, dst_ref=dst, send_sem=ss, recv_sem=rs, device_id=to, device_id_type=MESH
        )

    def cols(j, cc):
        return pl.ds(pl.multiple_of(j * 256 + cc * SH, SH), SH)

    loads = [
        pltpu.make_async_copy(w_in.at[0], W.at[idx(x, z), pl.ds(pl.multiple_of(c * SH, SH), SH)], load_sem.at[0]),
        pltpu.make_async_copy(op_in, opv, load_sem.at[1]),
        pltpu.make_async_copy(rp_in.at[0], rpv, load_sem.at[2]),
        pltpu.make_async_copy(g_in, gs.at[pl.ds(0, 384)], load_sem.at[3]),
        pltpu.make_async_copy(x_in, xv, load_sem.at[4]),
        pltpu.make_async_copy(mom_in, momv, load_sem.at[5]),
    ]
    for copy in loads[:4]:
        copy.start()

    barrier = pltpu.get_barrier_semaphore()
    peers = [sib, x_nb, outer, *z_nb]
    peers += [rep(xh, (y + j) % 4) for j in range(1, 4)]
    for peer in peers:
        pl.semaphore_signal(barrier, inc=1, device_id=peer, device_id_type=MESH)
    pl.semaphore_wait(barrier, len(peers))

    def rows(p, way):
        if p == 1:
            return HF, HF
        return 0, (LOW if p == 2 and way == 1 else HF)

    def wpiece(xx, zz, start, size, cc=None):
        cc = c if cc is None else cc
        return W.at[idx(xx, zz), pl.ds(pl.multiple_of(cc * SH + start, BLK), size)]

    def far(way, k):
        return zmod(z - k) if way == 0 else zmod(z + k)

    def ag_z(way, k, p, at):
        start, size = rows(p, way)
        ref = wpiece(ox if p == 2 else x, at, start, size)
        return remote(ref, ref, link_s.at[0], agz_r.at[way, k - 1, p], z_nb[way])

    def ag_z_send(way, k, p):
        ag_z(way, k, p, far(way, k - 1)).start()

    def ag_z_wait(way, k, p):
        ag_z(way, k, p, far(way, k)).wait_recv()

    def ag_x(n, zz, start, size):
        ref = wpiece(x, zz, start, size)
        return remote(ref, ref, link_s.at[0], agx_r.at[n], x_nb)

    def ag_x_wait(n, zz, start, size):
        ref = wpiece(ox, zz, start, size)
        remote(ref, ref, link_s.at[0], agx_r.at[n], x_nb).wait_recv()

    def ag_b_send(way, k):
        start = LOW if way == 1 else HF
        ag_x(1 + k, far(way, k), start, SH - start).start()

    def ag_b_wait(k):
        ref = W.at[idx(ox, far(0, k)), pl.ds(0, 2 * SH - LOW - HF if k < 4 else SH - LOW)]
        remote(ref, ref, link_s.at[0], agx_r.at[1 + k], x_nb).wait_recv()

    def sib_copy(xrel, o, cc):
        ref = wpiece(x if xrel == 0 else ox, zmod(z + o), 0, SH, cc)
        n = xrel * 5 + min(o, NZ - o)
        return remote(ref, ref, sib_s.at[0], sib_r.at[n], sib)

    def sib_wait(xrel, offsets):
        if len(offsets) == 1:
            sib_copy(xrel, offsets[0], oc).wait_recv()
        else:
            ref = W.at[idx(x if xrel == 0 else ox, zmod(z + offsets[0]))]
            remote(ref, ref, sib_s.at[0], sib_r.at[xrel * 5 + offsets[0]], sib).wait_recv()

    loads[0].wait()
    ag_x(0, z, 0, HF).start()
    for way in (0, 1):
        ag_z_send(way, 1, 0)
    ag_x(1, z, HF, HF).start()
    for way in (0, 1):
        ag_z_send(way, 1, 1)

    @pl.loop(0, 16)
    def _(j):
        at = pl.ds(pl.multiple_of(j * SH, SH), SH)
        remote(x_in.at[:, cols(j, oc)], xs.at[pl.ds(384, 384), at], tok_s.at[0], tok_r.at[0], sib).start()
        pltpu.make_async_copy(x_in.at[:, cols(j, c)], xs.at[pl.ds(0, 384), at], xs_sem.at[0]).start()

    tok_g = remote(g_in, gs.at[pl.ds(384, 384)], tok_s.at[1], tok_r.at[1], sib)
    tok_g.start()
    sib_copy(0, 0, c).start()
    loads[4].start()
    loads[5].start()

    loads[1].wait()
    loads[2].wait()

    @pl.loop(0, SH // BLK)
    def _(i):
        at = pl.ds(pl.multiple_of(i * BLK, BLK), BLK)
        diff[at, :] = opv[at, :] - rpv[at, :]

    def quarter(yy):
        return pl.ds(pl.multiple_of(yy * QT, QT), QT)

    def rep_scatter(j):
        to = (y + j) % 4
        return remote(diff.at[quarter(to)], ryv.at[j - 1], rep_s.at[0], rep_r.at[0], rep(xh, to))

    for j in range(1, 4):
        rep_scatter(j).start()

    def use(xrel, *offsets):
        sib_wait(xrel, offsets)
        first, step = offsets[0], offsets[-1] - offsets[0]

        @pl.loop(0, len(offsets))
        def _(t):
            i = idx(x if xrel == 0 else ox, zmod(z + first + t * step))
            at = pl.ds(pl.multiple_of(i * 256, 256), 256)
            w = W[i]
            dx_out[:, at] = lax.dot_general(
                gs[pl.ds(0, 384), :], w, (((1,), (1,)), ((), ())), preferred_element_type=F32
            ).astype(BF16)
            acc[...] += jnp.dot(xv[:, at], w, preferred_element_type=F32)

    acc[...] = jnp.zeros_like(acc)
    loads[3].wait()
    loads[4].wait()
    use(0, 0)

    ag_x_wait(0, z, 0, HF)
    for way in (0, 1):
        ag_z_send(way, 1, 2)

    tok_x = remote(xs.at[pl.ds(384, 384)], xs.at[pl.ds(384, 384)], tok_s.at[0], tok_r.at[0], sib)
    pltpu.make_async_copy(xs.at[pl.ds(0, 384)], xs.at[pl.ds(0, 384)], xs_sem.at[0]).wait()
    tok_g.wait_recv()
    tok_x.wait_recv()

    def partial(first, last):
        @pl.loop(first, last)
        def _(i):
            at = pl.ds(pl.multiple_of(i * 512, 512), 512)
            part[pl.ds(i * 4, 4)] = lax.dot_general(
                xs[:, at], gs[...], (((0,), (0,)), ((), ())), preferred_element_type=F32
            ).reshape(4, SH, 1024)

    def forward(k, p):
        for way in (0, 1):
            ag_z_wait(way, k, p)
            if k < 3 or (way, p) in ((0, 0), (1, 1), (1, 2)):
                ag_z_send(way, k + 1, p)
            if p == 1:
                ag_b_send(way, k)

    def off(way, k):
        return (NZ - k) % NZ if way == 0 else k

    def to_sib(k):
        for way in (0, 1):
            sib_copy(0, off(way, k), c).start()

    def to_sib_other(k):
        ag_b_wait(k)
        for way in (0, 1):
            sib_copy(1, off(way, k), c).start()

    partial(0, 1)
    forward(1, 0)
    partial(1, 2)
    forward(1, 1)
    to_sib(1)

    remote(ryv, ryv, rep_s.at[0], rep_r.at[0], outer).wait_recv()
    tot[quarter(y), :] = ((diff[quarter(y), :] + ryv[0]) + ryv[1]) + ryv[2]
    xhv[0] = tot[quarter(y), :]
    rep_out = remote(xhv.at[0], xhv.at[1], rep_s.at[0], rep_r.at[1], outer)
    rep_out.start()
    partial(2, 4)
    forward(1, 2)

    ag_x_wait(1, z, HF, HF)
    sib_copy(1, 0, c).start()

    def largest(i, m):
        v = jnp.abs(part[i // 2, pl.ds(pl.multiple_of((i % 2) * HF, HF), HF), :])
        for j in range(HF // 8):
            m = jnp.maximum(m, v[8 * j : 8 * j + 8])
        return m

    wide = lax.fori_loop(0, 32, largest, jnp.zeros((8, 1024), F32))
    narrow = wide[:, 0:128]
    for j in range(1, 8):
        narrow = jnp.maximum(narrow, wide[:, j * 128 : (j + 1) * 128])

    def top_copy(n, to):
        return remote(tq.at[n], tr.at[n], top_s.at[0], top_r.at[n], to)

    tq[8] = narrow
    top_copy(8, x_nb).start()

    def tile(m):
        return jnp.maximum(jnp.full((8, 128), jnp.max(m), F32), 1e-30)

    own_scale = jnp.max(2048.0 / tile(narrow))

    def encoded(dst, xx, zz, start, size, factor, received):
        @pl.loop(0, size // BLK)
        def _(i):
            at = pl.multiple_of(i * BLK, BLK)
            dst[pl.ds(at, BLK), :] = encode(total(xx, zz, start, at, factor, received))

    def total(xx, zz, start, at, factor, received):
        v = part[idx(xx, zz), pl.ds(pl.multiple_of(start + at, BLK), BLK), :] * factor
        for ref, by in received:
            w = decode(ref[pl.ds(pl.multiple_of(at, BLK), BLK), :])
            v = v + w * by
        return v

    def rs_x(n):
        return remote(xq.at[n], xr.at[n], link_s.at[0], rsx_r.at[n if n < 5 else NZ - n if n < NZ else 5], x_nb)

    def rs_x_wait(o):
        ref = xr.at[o] if o in (0, 4, 8) else xr.at[pl.ds(0, 2)]
        remote(ref, ref, link_s.at[0], rsx_r.at[o if o < 5 else 5], x_nb).wait_recv()

    def rs_b_send(o):
        encoded(xq.at[o], ox, zmod(z + o), HF, HF, own_scale, [])
        rs_x(o).start()

    def rs_z(way, j, p):
        here, there = zq.at[way, j, p], zr.at[way, j, p]
        return remote(here, there, link_s.at[0], rsz_r.at[way, j, p], z_nb[way])

    factors = {}

    def prepare(way, j):
        top, came = jnp.maximum(tq[8], tr[8]), None
        if j > 0:
            top_copy(way * 4 + j - 1, z_nb[way]).wait_recv()
            came = tr[way * 4 + j - 1]
            top = jnp.maximum(top, came)
        tq[way * 4 + j] = top
        top_copy(way * 4 + j, z_nb[way]).start()
        whole = tile(top)
        factors[way, j] = (
            jnp.max(2048.0 / whole),
            jnp.max(tile(tr[8]) / whole),
            None if came is None else jnp.max(tile(came) / whole),
        )

    def rs_send(way, j, p):
        o = 4 - j if way == 0 else (4 + j) % NZ
        zz, col = zmod(z + o), (ox if p == 2 else x)
        out, crossed = zq.at[way, j, p], xr.at[o]
        scale, by_x, by_z = factors[way, j]
        start, received = (HF, [(crossed, by_x)]) if p == 1 else (0, [])
        if j > 1 or (j == 1 and (way, p) in FIRST):
            rs_z(way, j - 1, p).wait_recv()
            received.append((zr.at[way, j - 1, p], by_z))
        encoded(out, col, zz, start, HF, scale, received)
        rs_z(way, j, p).start()

    for o in (4, 3, 5):
        rs_b_send(o)
    use(1, 0)
    forward(2, 0)
    use(0, 1, 7)
    forward(2, 1)
    to_sib(2)
    top_copy(8, x_nb).wait_recv()
    for way in (0, 1):
        prepare(way, 0)
    rs_send(0, 0, 0)
    rs_send(1, 0, 2)
    to_sib_other(1)
    forward(2, 2)
    rs_x_wait(4)
    rs_send(1, 0, 1)
    use(1, 1, 7)
    for way in (0, 1):
        prepare(way, 1)
    rs_send(0, 1, 2)
    rs_send(1, 1, 0)
    rep_out.wait_recv()
    rep_in = remote(xhv.at[1], xhv.at[2], rep_s.at[0], rep_r.at[3], x_nb)
    rep_in.start()
    for o in (2, 6):
        rs_b_send(o)
    use(0, 2, 6)

    rs_send(0, 1, 0)
    rs_send(1, 1, 2)
    rs_x_wait(3)
    for way in (0, 1):
        rs_send(way, 1, 1)
    forward(3, 0)
    to_sib_other(2)
    forward(3, 1)
    to_sib(3)
    use(1, 2, 6)
    forward(3, 2)
    for way in (0, 1):
        prepare(way, 2)
    rs_send(0, 2, 2)
    rs_send(1, 2, 0)
    for o in (1, 7):
        rs_b_send(o)
    rs_send(0, 2, 0)
    rs_send(1, 2, 2)
    use(0, 3, 5)
    rs_x_wait(2)
    for way in (0, 1):
        rs_send(way, 2, 1)

    rep_in.wait_recv()
    tot[quarter(y), :] = xhv[0] + xhv[2]

    def rep_gather(j, at):
        ref = tot.at[quarter(at)]
        return remote(ref, ref, rep_s.at[0], rep_r.at[2], rep(xh, (y + j) % 4))

    for j in range(1, 4):
        rep_gather(j, y).start()

    ag_z_wait(0, 4, 0)
    ag_z_wait(1, 4, 1)
    ag_b_send(1, 4)
    sib_copy(0, 4, c).start()
    ag_z_wait(1, 4, 2)
    rs_b_send(0)

    for way in (0, 1):
        prepare(way, 3)
    rs_send(0, 3, 2)
    rs_send(1, 3, 2)
    to_sib_other(3)
    rs_send(0, 3, 0)
    rs_send(1, 3, 0)
    use(1, 3, 5)
    rs_x_wait(1)
    for way in (0, 1):
        rs_send(way, 3, 1)
    use(0, 4)
    ag_b_wait(4)
    sib_copy(1, 4, c).start()

    loads[5].wait()
    remote(ryv, ryv, rep_s.at[0], rep_r.at[2], outer).wait_recv()

    @pl.loop(0, SH // BLK)
    def _(i):
        at = pl.ds(pl.multiple_of(i * BLK, BLK), BLK)
        outer = tot[at, :] * 0.125
        new = 0.9 * momv[at, :] + outer
        nm_out[at, :] = new
        np_out[at, :] = opv[at, :] - 0.7 * (outer + 0.9 * new)

    last = jnp.maximum(tq[8], tr[8])
    for way in (0, 1):
        top_copy(way * 4 + 3, z_nb[way]).wait_recv()
        last = jnp.maximum(last, tr[way * 4 + 3])
    tq[9] = last
    top_copy(9, x_nb).start()
    whole = tile(last)
    by_way = [jnp.max(tile(tr[way * 4 + 3]) / whole) for way in (0, 1)]
    for way in (0, 1):
        rs_z(way, 3, 2).wait_recv()
    encoded(xq.at[8], ox, z, 0, HF, jnp.max(2048.0 / whole), [(zr.at[way, 3, 2], by_way[way]) for way in (0, 1)])
    rs_x(8).start()

    def finish(start, received, add):
        @pl.loop(0, HF // BLK)
        def _(i):
            at = pl.multiple_of(i * BLK, BLK)
            out = pl.ds(pl.multiple_of(start + at, BLK), BLK)
            v = dw_out[0, out, :] if add else part[idx(x, z), out, :] * grad_scale
            for ref, by in received:
                v = v + decode(ref[pl.ds(at, BLK), :]) * by
            dw_out[0, out, :] = v

    def back(n):
        return jnp.max(tile(tr[n]) * (grad_scale / 2048.0))

    back_z = [back(way * 4 + 3) for way in (0, 1)]
    rs_x_wait(0)
    finish(HF, [(xr.at[0], back(8))], False)
    for way in (0, 1):
        rs_z(way, 3, 0).wait_recv()
    finish(0, [(zr.at[way, 3, 0], back_z[way]) for way in (0, 1)], False)
    use(1, 4)
    val_out[...] = acc[...].astype(BF16)
    top_copy(9, x_nb).wait_recv()
    back_x = back(9)
    for way in (0, 1):
        rs_z(way, 3, 1).wait_recv()
    finish(HF, [(zr.at[way, 3, 1], back_z[way]) for way in (0, 1)], True)
    rs_x_wait(8)
    finish(0, [(xr.at[8], back_x)], True)

    pieces = W.at[pl.ds(0, 15)]
    remote(pieces, pieces, link_s.at[0], top_r.at[0], x_nb).wait_send()
    pieces = W.at[pl.ds(0, 8)]
    remote(pieces, pieces, sib_s.at[0], top_r.at[0], sib).wait_send()
    tok_x.wait_send()
    tok_g.wait_send()
    remote(tr, tr, top_s.at[0], top_r.at[0], x_nb).wait_send()
    pieces = part.at[pl.ds(0, 8), pl.ds(0, QT)]
    remote(pieces, pieces, rep_s.at[0], top_r.at[0], outer).wait_send()


def store(*refs):
    sems = refs[10]
    copies = [pltpu.make_async_copy(refs[i], refs[5 + i], sems.at[i]) for i in (0, 2, 3, 4)]
    step = refs[1].shape[0] // 4
    for n in range(4):
        at = pl.ds(n * step, step)
        copies.insert(0, pltpu.make_async_copy(refs[1].at[at], refs[6].at[at], sems.at[5 + n]))
    for copy in copies:
        copy.start()
    for copy in copies:
        copy.wait()


def local(grad_scale, activations, cotangent, inner_weight, outer_params, replica_params, momentum):
    tokens, width = activations.shape
    kv = cotangent.shape[1]
    any_spec = pl.BlockSpec(memory_space=pl.ANY)
    vmem_spec = pl.BlockSpec(memory_space=pltpu.VMEM)
    dma = pltpu.SemaphoreType.DMA
    vm = pltpu.VMEM
    results = pl.pallas_call(
        functools.partial(kernel, grad_scale),
        out_shape=(
            vm((tokens, kv), BF16),
            vm((tokens, width), BF16),
            vm((1, SH, kv), F32),
            vm((SH, kv), F32),
            vm((SH, kv), F32),
        ),
        in_specs=[any_spec] * 6,
        out_specs=(vmem_spec,) * 5,
        scratch_shapes=[
            vm((tokens, width), BF16),
            vm((2 * tokens, width // 2), BF16),
            vm((2 * tokens, kv), BF16),
            vm((16, 2 * SH, kv), BF16),
            vm((16, SH, kv), F32),
            vm((2, 4, 3, HF, kv), BF16),
            vm((2, 4, 3, HF, kv), BF16),
            vm((9, HF, kv), BF16),
            vm((9, HF, kv), BF16),
            vm((tokens, kv), F32),
            vm((SH, kv), F32),
            vm((SH, kv), F32),
            vm((SH, kv), F32),
            vm((SH, kv), F32),
            vm((3, QT, kv), F32),
            vm((3, QT, kv), F32),
            vm((SH, kv), F32),
            vm((10, 8, 128), F32),
            vm((10, 8, 128), F32),
            dma((6,)), dma((1,)), dma((2,)), dma((2,)),
            dma((1,)), dma((1,)), dma((1,)), dma((1,)),
            dma((2, 4, 3)), dma((6,)), dma((10,)), dma((2, 4, 3)), dma((6,)), dma((10,)), dma((4,)),
        ],
        compiler_params=pltpu.CompilerParams(
            collective_id=0, has_side_effects=True, vmem_limit_bytes=57 << 20
        ),
        name="step",
    )(activations, cotangent, inner_weight, outer_params, replica_params, momentum)
    return pl.pallas_call(
        store,
        out_shape=[jax.ShapeDtypeStruct(v.shape, v.dtype) for v in results],
        in_specs=[vmem_spec] * 5,
        out_specs=[pl.BlockSpec(memory_space=pltpu.HBM)] * 5,
        scratch_shapes=[dma((9,))],
        compiler_params=pltpu.CompilerParams(vmem_limit_bytes=1 << 20),
        name="store",
    )(*[pltpu.with_memory_space_constraint(v, pltpu.VMEM) for v in results])


def solution(mesh):
    rows = P(("replica", "fsdp"), None)
    placed = (rows, rows, P("replica", "fsdp", None), P("fsdp", None), P("replica", "fsdp", None), P("fsdp", None))

    def run(activations, *rest):
        grad_scale = 1.0 / math.sqrt(activations.shape[0] // mesh.shape["replica"])
        return jax.shard_map(
            functools.partial(local, grad_scale),
            mesh=mesh,
            in_specs=placed,
            out_specs=(rows, rows, P("replica", "fsdp", None), P("fsdp", None), P("fsdp", None)),
            check_vma=False,
        )(activations, *rest)

    return run
```
